768 devices in a mesh: wide: 64 (over y, x, core), narrow: 12 (over z).
Axes of the slice: x: 4, y: 8, z: 12, core: 2. Of those that a mesh axis runs over, the one named last changes fastest.
Arguments:
- features: bfloat16 [393216, 1024], P(('wide', 'narrow')), may hold values from -6 to 6
- stale_store: bfloat16 [196608, 1024], P(('wide', 'narrow')), may hold values from -6 to 6
- serve_rows: int32 [49152, 8], P(('wide', 'narrow')), may hold values from 0 to 255
- neighbours: int32 [393216, 8], P(('wide', 'narrow')), may hold values from 0 to 1023
- degrees: int32 [393216], P(('wide', 'narrow')), may hold values from 1 to 8
- push_rows: int32 [196608], P(('wide', 'narrow')), may hold values from 0 to 511
- weight: bfloat16 [1024, 1024], replicated, may hold values from -0.1875 to 0.1875
- cotangent: bfloat16 [393216, 1024], P(('wide', 'narrow')), may hold values from -6 to 6
Outputs:
- refreshed_store: bfloat16 [196608, 1024], P(('wide', 'narrow'))
- grad_weight: float32 [1024, 1024], P('wide')
The draws below stay inside these ranges and needn't reach their ends.
Inputs may be any that keep to these rules, and one draw needn't show every extreme that they name: `serve_rows`: A row number within the owner device's store rows. `neighbours`: A value below 512 names a node of the same device; 512 + p * 8 + q names slot q of the block pulled from partition p. Only the first degrees entries of a node are read. `push_rows`: A node of the same device.
All inputs are finite; a program needn't handle non-finite values.
Results may differ from the reference program's by a relative error of at most 0.0053.
Values may be sent and summed in bfloat16 or wider, within the bound.
A program may use at most 64 MiB of HBM per device.

```python
import math
import jax
import jax.numpy as jnp
from jax import lax

H = 1024
ROWS_DEV = 512
STORE_DEV = 256
PULL = 8
DEG = 8
NODES = 393216
STORE_ROWS = 196608
N_WIDE = 64
N_NARROW = 12


def touch_ends(values, rng, low, top_value):
    place = [jax.random.randint(jax.random.fold_in(rng, axis), (), 0, length) for axis, length in enumerate(values.shape)]
    widest = values.shape.index(max(values.shape))
    neighbour = place[:widest] + [(place[widest] + 1) % values.shape[widest]] + place[widest + 1:]
    return values.at[tuple(place)].set(low).at[tuple(neighbour)].set(top_value)


def level_of(own_key, shape, pieces, low, high):
    def one(dim, blocks):
        draws = jax.random.uniform(jax.random.fold_in(jax.random.fold_in(own_key, 6), dim), (blocks,), jnp.float32, low / len(pieces), high / len(pieces))
        return jnp.repeat(jnp.exp(draws), shape[dim] // blocks).reshape((-1,) + (1,) * (len(shape) - dim - 1))

    factor_of = one(*pieces[0])
    for cut in pieces[1:]:
        factor_of = factor_of * one(*cut)
    return factor_of


def bell_draw(own_key, shape, deviation, most, split=(), kind=jnp.bfloat16):
    factor_of = level_of(own_key, shape, split, -0.22, 0.18) if split else 1.0
    result = jax.random.normal(own_key, shape, jnp.float32) * deviation * factor_of
    return jnp.minimum(jnp.maximum(result, -most), most).astype(kind)


def setup_inputs(seed: int = 0) -> dict:
    key_list = jax.random.split(jax.random.key(seed), 9)
    return {
        "features": bell_draw(key_list[0], (NODES, H), 1.0, 6.0, ((0, 768),)),
        "stale_store": bell_draw(key_list[1], (STORE_ROWS, H), 1.0, 6.0, ((0, 768),)),
        "serve_rows": touch_ends(jax.random.randint(key_list[2], (N_WIDE * N_NARROW * N_WIDE, PULL), 0, STORE_DEV), jax.random.fold_in(key_list[2], 1), 0, STORE_DEV - 1).astype(jnp.int32),
        "neighbours": touch_ends(jax.random.randint(key_list[3], (NODES, DEG), 0, ROWS_DEV + N_WIDE * PULL), jax.random.fold_in(key_list[3], 1), 0, (ROWS_DEV + N_WIDE * PULL) - 1).astype(jnp.int32),
        "degrees": touch_ends(jax.random.randint(key_list[4], (NODES,), 1, DEG + 1), jax.random.fold_in(key_list[4], 1), 1, DEG).astype(jnp.int32),
        "push_rows": touch_ends(jax.random.randint(key_list[5], (STORE_ROWS,), 0, ROWS_DEV), jax.random.fold_in(key_list[5], 1), 0, ROWS_DEV - 1).astype(jnp.int32),
        "weight": bell_draw(key_list[6], (H, H), H ** -0.5, 0.1875),
        "cotangent": bell_draw(key_list[7], (NODES, H), 1.0, 6.0, ((0, 768),)),
    }


def reference(features, stale_store, serve_rows, neighbours, degrees, push_rows, weight, cotangent):
    wide_size = N_WIDE
    narrow_size = N_NARROW
    device_count = wide_size * narrow_size
    feature_blocks = features.reshape(device_count, ROWS_DEV, H)
    store_blocks = stale_store.reshape(wide_size, narrow_size, STORE_DEV, H)
    serve_blocks = serve_rows.reshape(wide_size, narrow_size, wide_size, PULL)
    neighbour_blocks = neighbours.reshape(device_count, ROWS_DEV, DEG)
    degree_blocks = degrees.reshape(device_count, ROWS_DEV)
    push_blocks = push_rows.reshape(device_count, STORE_DEV)
    cotangent_blocks = cotangent.reshape(device_count, ROWS_DEV, H)

    def per_device(gradient, inputs):
        device, own_rows, own_nbrs, own_degrees, own_push, own_cot = inputs
        part_index = (device // narrow_size).astype(jnp.int32)
        range_index = (device % narrow_size).astype(jnp.int32)
        shards = lax.dynamic_index_in_dim(store_blocks, range_index, 1, keepdims=False)
        serve_range = lax.dynamic_index_in_dim(serve_blocks, range_index, 1, keepdims=False)
        wanted = lax.dynamic_index_in_dim(serve_range, part_index, 1, keepdims=False)
        pulled = jnp.take_along_axis(shards, wanted[:, :, None], axis=1).reshape(wide_size * PULL, H)
        lookup_table = jnp.concatenate([own_rows, pulled], axis=0)
        picked = lookup_table[own_nbrs].astype(jnp.float32)
        active = jnp.arange(DEG, dtype=jnp.int32)[None, :] < own_degrees[:, None]
        summed = lax.optimization_barrier(jnp.sum(jnp.where(active[:, :, None], picked, jnp.float32(0.0)), axis=1))
        agg = ((own_rows.astype(jnp.float32) + summed) / (own_degrees.astype(jnp.float32) + 1.0)[:, None]).astype(jnp.bfloat16)
        preact = jnp.dot(agg, weight, preferred_element_type=jnp.float32)
        sigma_value = jax.nn.sigmoid(preact)
        output_rows = (preact * sigma_value).astype(jnp.bfloat16)
        refreshed = output_rows[own_push]
        grad_pre = (own_cot.astype(jnp.float32) * sigma_value * (1.0 + preact * (1.0 - sigma_value))).astype(jnp.bfloat16)
        partial_term = jnp.dot(agg.T, grad_pre, preferred_element_type=jnp.float32)
        return (gradient + partial_term, refreshed)
    device_ids = jnp.arange(device_count, dtype=jnp.int32)
    gradient, refreshed = lax.scan(per_device, jnp.zeros((H, H), jnp.float32), (device_ids, feature_blocks, neighbour_blocks, degree_blocks, push_blocks, cotangent_blocks))
    gradient = gradient * (1.0 / math.sqrt(device_count * ROWS_DEV))
    return (refreshed.reshape(device_count * STORE_DEV, H), gradient)
```

```python
import functools
import math

import jax
import jax.numpy as jnp
from jax import lax
from jax.experimental import pallas as pl
from jax.experimental.pallas import tpu as pltpu
from jax.sharding import PartitionSpec as P

MESH = pl.DeviceIdType.MESH
F32 = jnp.float32
BF16 = jnp.bfloat16

NY, NX, NC = 8, 4, 2
NCH = 4
SCALE = 1.0 / math.sqrt(393216)


def iota(shape, dim):
    return lax.broadcasted_iota(jnp.int32, shape, dim)


def centre_out(k, half):
    return half + (1 - 2 * (k % 2)) * ((k + 1) // 2)


def kernel(
    features, store, serve_t, neigh_t, degrees, push, weight, cotangent,
    refreshed, grad_out,
    store_v, feat_v, weight_v, cot_v, outgoing, pulled, a_pull, acc, cols_v, push_v,
    agg, agg_t, agg_t_peer, out_v, dz, dz_peer, part,
    x_send, x_recv, y_send, y_recv, z_recv, refreshed_v,
    in_sem, pull_s, pull_r, core_s, core_r, xs, xr, ys, yr, zs, zr, out_sem,
):
    w = lax.axis_index("wide")
    n = lax.axis_index("narrow")
    nw, nz = NY * NX * NC, 12
    y, x, c = w // (NX * NC), (w // NC) % NX, w % NC
    rows, width = feat_v.shape
    cw = width // NCH

    loads = [
        pltpu.make_async_copy(src, dst, in_sem.at[i])
        for i, (src, dst) in enumerate(
            [(store, store_v), (features, feat_v), (weight, weight_v), (cotangent, cot_v)]
        )
    ]
    for load in loads:
        load.start()

    barrier = pltpu.get_barrier_semaphore()

    @pl.loop(1, nw)
    def _(j):
        pl.semaphore_signal(barrier, inc=1, device_id=((w + j) % nw, n), device_id_type=MESH)

    @pl.loop(1, nz)
    def _(j):
        pl.semaphore_signal(barrier, inc=1, device_id=(w, (n + j) % nz), device_id_type=MESH)

    slots = nw * 8
    tiled = jnp.tile(serve_t[...].astype(F32), (nw, 1))
    mine = iota((slots, nw), 1) == iota((slots, nw), 0) // 8
    wanted = jnp.sum(jnp.where(mine, tiled, 0.0), axis=1, keepdims=True)
    pick = (wanted.astype(jnp.int32) == iota((slots, store_v.shape[0]), 1)).astype(F32).astype(BF16)
    loads[0].wait()
    outgoing[...] = (
        jnp.dot(pick, store_v[...], preferred_element_type=F32).astype(BF16).reshape(nw, 8, width)
    )

    pl.semaphore_wait(barrier, nw - 1 + nz - 1)

    def pull_copy(j):
        dy = centre_out(j // (NX * NC), NY // 2)
        dx = centre_out((j // NC) % NX, NX // 2)
        dc = 1 - j % NC
        p = (((y + dy) % NY) * NX + (x + dx) % NX) * NC + (c + dc) % NC
        return p

    @pl.loop(0, nw - 1)
    def _(j):
        p = pull_copy(j)
        pltpu.make_async_remote_copy(
            src_ref=outgoing.at[p], dst_ref=pulled.at[w], send_sem=pull_s.at[p], recv_sem=pull_r.at[w],
            device_id=(p, n), device_id_type=MESH,
        ).start()

    pulled[w] = outgoing[w]
    deg = degrees[...]
    live = iota((8, rows), 0) < deg
    idx = jnp.where(live, neigh_t[...], -1).astype(F32)
    deg1 = jnp.broadcast_to(deg.astype(F32) + 1.0, (8, rows))
    pushed = jnp.concatenate([push[...].astype(F32)] * 2, axis=1)
    pushed = jnp.broadcast_to(pushed, (8, rows))
    stacked = jnp.concatenate([idx, deg1, pushed, jnp.zeros((104, rows), F32)], axis=0)
    cols_v[...] = stacked.T
    loads[1].wait()

    step = 64

    @pl.loop(0, rows // step)
    def _(b):
        r = pl.ds(pl.multiple_of(b * step, step), step)
        cols = cols_v[r, :].astype(jnp.int32)
        near = jnp.zeros((step, rows), F32)
        far = jnp.zeros((step, slots), F32)
        for k in range(8):
            col = cols[:, k : k + 1]
            near = near + (col == iota((step, rows), 1)).astype(F32)
            far = far + (col == iota((step, slots), 1) + rows).astype(F32)
        a_pull[r, :] = far.astype(BF16)
        acc[r, :] = feat_v[r, :].astype(F32) + jnp.dot(
            near.astype(BF16), feat_v[...], preferred_element_type=F32
        )

    push_v[...] = (
        (cols_v[0 : push_v.shape[0], 16:17].astype(jnp.int32) == iota(push_v.shape, 1)).astype(F32).astype(BF16)
    )
    loads[2].wait()
    loads[3].wait()

    @pl.loop(0, nw - 1)
    def _(j):
        p = pull_copy(j)
        pltpu.make_async_remote_copy(
            src_ref=outgoing.at[p], dst_ref=pulled.at[p], send_sem=pull_s.at[p], recv_sem=pull_r.at[p],
            device_id=(p, n), device_id_type=MESH,
        ).wait_recv()

    total = acc[...] + jnp.dot(
        a_pull[...], pulled[...].reshape(slots, width), preferred_element_type=F32
    )
    agg[...] = (total / cols_v[:, 8:9]).astype(BF16)
    agg_t[...] = agg[...].T.reshape(nw // NC, NC, 16, rows)

    other = (y * NX + x) * NC + 1 - c

    def core_copy(src, dst, i):
        return pltpu.make_async_remote_copy(
            src_ref=src, dst_ref=dst, send_sem=core_s.at[i], recv_sem=core_r.at[i],
            device_id=(other, n), device_id_type=MESH,
        )

    core = [core_copy(agg_t.at[:, 1 - c], agg_t_peer, NCH)]
    core[0].start()
    for h in range(NCH):
        at = pl.ds(h * cw, cw)
        z = jnp.dot(agg[...], weight_v[:, at], preferred_element_type=F32)
        s = jax.nn.sigmoid(z)
        out_v[:, at] = (z * s).astype(BF16)
        dz[h] = (cot_v[:, at].astype(F32) * s * (1.0 + z * (1.0 - s))).astype(BF16)
        copy = core_copy(dz.at[h], dz_peer.at[h], h)
        copy.start()
        core.append(copy)

    core[0].wait_recv()
    mine_t = agg_t[:, c].reshape(rows, rows)
    peer_t = agg_t_peer[...].reshape(rows, rows)

    def x_copy(h, d, there):
        px = (x + d) % NX
        return pltpu.make_async_remote_copy(
            src_ref=x_send.at[h, px], dst_ref=x_recv.at[h, x if there else px],
            send_sem=xs.at[h, px], recv_sem=xr.at[h, x if there else px],
            device_id=((y * NX + px) * NC + c, n), device_id_type=MESH,
        )

    def y_copy(h, d, there):
        py = (y + d) % NY
        return pltpu.make_async_remote_copy(
            src_ref=y_send.at[h, py], dst_ref=y_recv.at[h, y if there else py],
            send_sem=ys.at[h, py], recv_sem=yr.at[h, y if there else py],
            device_id=((py * NX + x) * NC + c, n), device_id_type=MESH,
        )

    def z_copy(h, d, there):
        pz = (n + d) % nz
        return pltpu.make_async_remote_copy(
            src_ref=z_recv.at[h, n], dst_ref=z_recv.at[h, n if there else pz],
            send_sem=zs.at[h, pz], recv_sem=zr.at[h, n if there else pz],
            device_id=(w, pz), device_id_type=MESH,
        )

    far_x, far_y = (2, 1, 3), (4, 3, 5, 2, 6, 1, 7)
    far_z = (6, 5, 7, 4, 8, 3, 9, 2, 10, 1, 11)
    for h in range(NCH):
        core[1 + h].wait_recv()
        g = jnp.dot(mine_t, dz[h], preferred_element_type=F32) + jnp.dot(
            peer_t, dz_peer[h], preferred_element_type=F32
        )
        part[h] = g.reshape(NY, NX, 16, cw)
        for k in range(NX):
            x_send[h, k] = part[h, :, k].astype(BF16)
        for d in far_x:
            x_copy(h, d, True).start()

    for h in range(NCH):
        at = pl.ds(h * cw, cw)
        refreshed_v[:, at] = jnp.dot(
            push_v[...], out_v[:, at], preferred_element_type=F32
        ).astype(BF16)
    store_back = pltpu.make_async_copy(refreshed_v, refreshed, out_sem)
    store_back.start()

    for h in range(NCH):
        for d in far_x:
            x_copy(h, d, False).wait_recv()
        total = part[h, :, x]
        for d in far_x:
            total = total + x_recv[h, (x + d) % NX].astype(F32)
        part[h, :, 0] = total
        y_send[h] = total.astype(BF16)
        for d in far_y:
            y_copy(h, d, True).start()

    for h in range(NCH):
        for d in far_y:
            y_copy(h, d, False).wait_recv()
        total = part[h, y, 0]
        for d in far_y:
            total = total + y_recv[h, (y + d) % NY].astype(F32)
        z_recv[h, n] = total.astype(BF16)
        for d in far_z:
            z_copy(h, d, True).start()

    for h in range(NCH):
        for d in far_z:
            z_copy(h, d, False).wait_recv()
        total = z_recv[h, 0].astype(F32)
        for k in range(1, nz):
            total = total + z_recv[h, k].astype(F32)
        grad_out[:, pl.ds(h * cw, cw)] = total * F32(SCALE)

    @pl.loop(0, nw - 1)
    def _(j):
        p = pull_copy(j)
        pltpu.make_async_remote_copy(
            src_ref=outgoing.at[p], dst_ref=pulled.at[p], send_sem=pull_s.at[p], recv_sem=pull_r.at[p],
            device_id=(p, n), device_id_type=MESH,
        ).wait_send()

    for copy in core:
        copy.wait_send()
    for h in range(NCH):
        for d in far_x:
            x_copy(h, d, True).wait_send()
        for d in far_y:
            y_copy(h, d, True).wait_send()
        for d in far_z:
            z_copy(h, d, True).wait_send()
    store_back.wait()


def local(features, stale_store, serve_rows, neighbours, degrees, push_rows, weight, cotangent):
    rows, width = features.shape
    stores = stale_store.shape[0]
    nw, nz = NY * NX * NC, 12
    cw = width // NCH
    any_, vmem = pl.BlockSpec(memory_space=pl.ANY), pl.BlockSpec(memory_space=pltpu.VMEM)
    dma = pltpu.SemaphoreType.DMA
    V = pltpu.VMEM
    return pl.pallas_call(
        kernel,
        out_shape=(
            jax.ShapeDtypeStruct((stores, width), BF16),
            jax.ShapeDtypeStruct((width // nw, width), F32),
        ),
        in_specs=[any_, any_, vmem, vmem, vmem, vmem, any_, any_],
        out_specs=(any_, vmem),
        scratch_shapes=[
            V((stores, width), BF16),
            V((rows, width), BF16),
            V((width, width), BF16),
            V((rows, width), BF16),
            V((nw, 8, width), BF16),
            V((nw, 8, width), BF16),
            V((rows, nw * 8), BF16),
            V((rows, width), F32),
            V((rows, 128), F32),
            V((stores, rows), BF16),
            V((rows, width), BF16),
            V((nw // NC, NC, 16, rows), BF16),
            V((nw // NC, 16, rows), BF16),
            V((rows, width), BF16),
            V((NCH, rows, cw), BF16),
            V((NCH, rows, cw), BF16),
            V((NCH, NY, NX, 16, cw), F32),
            V((NCH, NX, NY, 16, cw), BF16),
            V((NCH, NX, NY, 16, cw), BF16),
            V((NCH, NY, 16, cw), BF16),
            V((NCH, NY, 16, cw), BF16),
            V((NCH, nz, 16, cw), BF16),
            V((stores, width), BF16),
            dma((4,)),
            dma((nw,)),
            dma((nw,)),
            dma((NCH + 1,)),
            dma((NCH + 1,)),
            dma((NCH, NX)),
            dma((NCH, NX)),
            dma((NCH, NY)),
            dma((NCH, NY)),
            dma((NCH, nz)),
            dma((NCH, nz)),
            dma(()),
        ],
        compiler_params=pltpu.CompilerParams(
            collective_id=0, has_side_effects=True, vmem_limit_bytes=56 * 2**20
        ),
        cost_estimate=pl.CostEstimate(flops=6 * 10**9, bytes_accessed=6 * 2**20, transcendentals=2**20),
        name="sage",
    )(
        features, stale_store, serve_rows.T, neighbours.T, degrees.reshape(1, rows),
        push_rows.reshape(1, stores), weight, cotangent,
    )


def solution(mesh):
    both = P(("wide", "narrow"), None)
    flat = P(("wide", "narrow"))
    return jax.shard_map(
        local, mesh=mesh, in_specs=(both, both, both, both, flat, flat, P(), both),
        out_specs=(both, P("wide", None)), check_vma=False,
    )
```

```python
import functools
import math

import jax
import jax.numpy as jnp
from jax import lax
from jax.experimental import pallas as pl
from jax.experimental.pallas import tpu as pltpu
from jax.sharding import PartitionSpec as P

MESH = pl.DeviceIdType.MESH
F32 = jnp.float32
BF16 = jnp.bfloat16

NY, NX, NC = 8, 4, 2
NCH = 4
FIRST = 2
SCALE = 1.0 / math.sqrt(393216)


def iota(shape, dim):
    return lax.broadcasted_iota(jnp.int32, shape, dim)


def kernel(
    features, store, serve_t, neigh_t, degrees, push, weight, cotangent,
    refreshed, grad_out,
    store_v, feat_v, weight_v, cot_v, pick, outgoing, staged, pulled, a_pull, acc, cols_v, push_v,
    agg, agg_t, agg_t_peer, out_v, dz, dz_peer, part,
    x_send, x_recv, y_send, y_recv, z_recv, refreshed_v,
    in_sem, pull_s, pull_r, relay_s, relay_r, core_s, core_r, xs, xr, ys, yr, zs, zr, out_sem,
):
    w = lax.axis_index("wide")
    n = lax.axis_index("narrow")
    nw, nz = NY * NX * NC, 12
    y, x, c = w // (NX * NC), (w // NC) % NX, w % NC
    rows, width = feat_v.shape
    cw = width // NCH

    loads = [
        pltpu.make_async_copy(src, dst, in_sem.at[i])
        for i, (src, dst) in enumerate(
            [(store, store_v), (features, feat_v), (weight, weight_v), (cotangent, cot_v)]
        )
    ]
    for load in loads:
        load.start()

    barrier = pltpu.get_barrier_semaphore()

    def at_y(d):
        return (((y + d) % NY * NX + x) * NC + c, n)

    def at_xc(dx, dc):
        return ((y * NX + (x + dx) % NX) * NC + (c + dc) % NC, n)

    far_x, far_y = (2, 1, 3), (4, 3, 5, 2, 6, 1, 7)
    far_z = (6, 5, 7, 4, 8, 3, 9, 2, 10, 1, 11)
    others = [at_y(d) for d in far_y] + [(w, (n + d) % nz) for d in far_z]
    others += [at_xc(dx, dc) for dx in range(NX) for dc in range(NC) if dx or dc]
    for device in others:
        pl.semaphore_signal(barrier, inc=1, device_id=device, device_id_type=MESH)

    slots = nw * 8
    tiled = jnp.tile(serve_t[...].astype(F32), (nw, 1))
    s = iota((slots, nw), 0)
    reader = ((s // 16) % NY * NX + s // (NY * 16)) * NC + (s // 8) % NC
    wanted = jnp.sum(jnp.where(iota((slots, nw), 1) == reader, tiled, 0.0), axis=1, keepdims=True)
    hot = wanted.astype(jnp.int32) == iota((slots, store_v.shape[0]), 1)
    pick[...] = hot.astype(F32).astype(BF16).reshape(pick.shape)
    loads[0].wait()

    rounds = (2, 1, 3, 0)

    def pull_copy(r, d, there):
        px, py = (x + rounds[r]) % NX, (y + d) % NY
        to = y if there else py
        return pltpu.make_async_remote_copy(
            src_ref=outgoing.at[px, py], dst_ref=staged.at[px, :, to],
            send_sem=pull_s.at[r, py], recv_sem=pull_r.at[r, to],
            device_id=at_y(d), device_id_type=MESH,
        )

    def relay_copy(dx, dc, there):
        px, pc = (x + dx) % NX, (c + dc) % NC
        to = x * NC + c if there else px * NC + pc
        return pltpu.make_async_remote_copy(
            src_ref=staged.at[px, pc], dst_ref=pulled.at[to],
            send_sem=relay_s.at[px * NC + pc], recv_sem=relay_r.at[to],
            device_id=at_xc(dx, dc), device_id_type=MESH,
        )

    def serve(r):
        px = (x + rounds[r]) % NX
        rows_out = jnp.dot(pick[px], store_v[...], preferred_element_type=F32).astype(BF16)
        outgoing[px] = rows_out.reshape(NY, NC, 8, width)
        if r == 0:
            pl.semaphore_wait(barrier, len(others))
        for d in far_y:
            pull_copy(r, d, True).start()
        staged[px, :, y] = outgoing[px, y]

    def relay(r):
        for d in far_y:
            pull_copy(r, d, False).wait_recv()
        dx = rounds[r]
        for dc in range(NC):
            if dx or dc:
                relay_copy(dx, dc, True).start()
            else:
                pulled[x * NC + c] = staged[x, c]

    for r in range(FIRST):
        serve(r)

    deg = degrees[...]
    live = iota((8, rows), 0) < deg
    idx = jnp.where(live, neigh_t[...], -1).astype(F32)
    deg1 = jnp.broadcast_to(deg.astype(F32) + 1.0, (8, rows))
    pushed = jnp.concatenate([push[...].astype(F32)] * 2, axis=1)
    pushed = jnp.broadcast_to(pushed, (8, rows))
    stacked = jnp.concatenate([idx, deg1, pushed, jnp.zeros((104, rows), F32)], axis=0)
    cols_v[...] = stacked.T
    loads[1].wait()

    step = 64
    at = iota((step, slots), 1)
    named = rows + (at // 8 % NY * (NX * NC) + at // (8 * NY)) * 8 + at % 8

    @pl.loop(0, rows // step)
    def _(b):
        r = pl.ds(pl.multiple_of(b * step, step), step)
        cols = cols_v[r, :].astype(jnp.int32)
        near = jnp.zeros((step, rows), F32)
        far = jnp.zeros((step, slots), F32)
        for k in range(8):
            col = cols[:, k : k + 1]
            near = near + (col == iota((step, rows), 1)).astype(F32)
            far = far + (col == named).astype(F32)
        a_pull[r, :] = far.astype(BF16)
        acc[r, :] = feat_v[r, :].astype(F32) + jnp.dot(
            near.astype(BF16), feat_v[...], preferred_element_type=F32
        )

    push_v[...] = (
        (cols_v[0 : push_v.shape[0], 16:17].astype(jnp.int32) == iota(push_v.shape, 1)).astype(F32).astype(BF16)
    )
    loads[2].wait()
    loads[3].wait()

    for r in range(NX):
        relay(r)
        if r + FIRST < NX:
            serve(r + FIRST)
    for dx in range(NX):
        for dc in range(NC):
            if dx or dc:
                relay_copy(dx, dc, False).wait_recv()

    total = acc[...] + jnp.dot(
        a_pull[...], pulled[...].reshape(slots, width), preferred_element_type=F32
    )
    agg[...] = (total / cols_v[:, 8:9]).astype(BF16)
    agg_t[...] = agg[...].T.reshape(nw // NC, NC, 16, rows)

    other = (y * NX + x) * NC + 1 - c

    def core_copy(src, dst, i):
        return pltpu.make_async_remote_copy(
            src_ref=src, dst_ref=dst, send_sem=core_s.at[i], recv_sem=core_r.at[i],
            device_id=(other, n), device_id_type=MESH,
        )

    core = [core_copy(dz.at[h], dz_peer.at[h], h) for h in range(NCH)]
    core.append(core_copy(agg_t.at[:, 1 - c], agg_t_peer, NCH))
    core[NCH].start()

    def x_copy(h, d, there):
        px = (x + d) % NX
        return pltpu.make_async_remote_copy(
            src_ref=x_send.at[h, px], dst_ref=x_recv.at[h, x if there else px],
            send_sem=xs.at[h, px], recv_sem=xr.at[h, x if there else px],
            device_id=((y * NX + px) * NC + c, n), device_id_type=MESH,
        )

    def y_copy(h, d, there):
        py = (y + d) % NY
        return pltpu.make_async_remote_copy(
            src_ref=y_send.at[h, py], dst_ref=y_recv.at[h, y if there else py],
            send_sem=ys.at[h, py], recv_sem=yr.at[h, y if there else py],
            device_id=((py * NX + x) * NC + c, n), device_id_type=MESH,
        )

    def z_copy(h, d, there):
        pz = (n + d) % nz
        return pltpu.make_async_remote_copy(
            src_ref=z_recv.at[h, n], dst_ref=z_recv.at[h, n if there else pz],
            send_sem=zs.at[h, pz], recv_sem=zr.at[h, n if there else pz],
            device_id=(w, pz), device_id_type=MESH,
        )

    def forward(h):
        at = pl.ds(h * cw, cw)
        z = jnp.dot(agg[...], weight_v[:, at], preferred_element_type=F32)
        s = jax.nn.sigmoid(z)
        dz[h] = (cot_v[:, at].astype(F32) * s * (1.0 + z * (1.0 - s))).astype(BF16)
        core[h].start()
        out_v[:, at] = (z * s).astype(BF16)

    def backward(h):
        if h == 0:
            core[NCH].wait_recv()
        g = jnp.dot(agg_t[:, c].reshape(rows, rows), dz[h], preferred_element_type=F32)
        core[h].wait_recv()
        g = g + jnp.dot(agg_t_peer[...].reshape(rows, rows), dz_peer[h], preferred_element_type=F32)
        part[h] = g.reshape(NY, NX, 16, cw)
        for k in range(NX):
            x_send[h, k] = part[h, :, k].astype(BF16)
        for d in far_x:
            x_copy(h, d, True).start()

    def after_x(h):
        for d in far_x:
            x_copy(h, d, False).wait_recv()
        total = part[h, :, x]
        for d in far_x:
            total = total + x_recv[h, (x + d) % NX].astype(F32)
        part[h, :, 0] = total
        y_send[h] = total.astype(BF16)
        for d in far_y:
            y_copy(h, d, True).start()

    def after_y(h):
        for d in far_y:
            y_copy(h, d, False).wait_recv()
        total = part[h, y, 0]
        for d in far_y:
            total = total + y_recv[h, (y + d) % NY].astype(F32)
        z_recv[h, n] = total.astype(BF16)
        for d in far_z:
            z_copy(h, d, True).start()

    def after_z(h):
        for d in far_z:
            z_copy(h, d, False).wait_recv()
        total = z_recv[h, 0].astype(F32)
        for k in range(1, nz):
            total = total + z_recv[h, k].astype(F32)
        grad_out[:, pl.ds(h * cw, cw)] = total * F32(SCALE)

    forward(0)
    forward(1)
    backward(0)
    forward(2)
    backward(1)
    forward(3)
    backward(2)
    backward(3)

    after_x(0)
    for h in range(NCH):
        at = pl.ds(h * cw, cw)
        refreshed_v[:, at] = jnp.dot(
            push_v[...], out_v[:, at], preferred_element_type=F32
        ).astype(BF16)
    store_back = pltpu.make_async_copy(refreshed_v, refreshed, out_sem)
    store_back.start()

    after_x(1)
    after_y(0)

    for r in range(NX):
        for d in far_y:
            pull_copy(r, d, True).wait_send()
    for dx in range(NX):
        for dc in range(NC):
            if dx or dc:
                relay_copy(dx, dc, True).wait_send()

    after_x(2)
    after_y(1)
    after_x(3)
    after_y(2)
    after_z(0)
    for copy in core:
        copy.wait_send()
    for h in range(NCH):
        for d in far_x:
            x_copy(h, d, True).wait_send()
    after_y(3)
    after_z(1)
    for h in range(NCH):
        for d in far_y:
            y_copy(h, d, True).wait_send()
    after_z(2)
    store_back.wait()
    after_z(3)
    for h in range(NCH):
        for d in far_z:
            z_copy(h, d, True).wait_send()


def finish(refreshed, grad, refreshed_out, grad_out, sem):
    copies = [
        pltpu.make_async_copy(refreshed, refreshed_out, sem.at[0]),
        pltpu.make_async_copy(grad, grad_out, sem.at[1]),
    ]
    for copy in copies:
        copy.start()
    for copy in copies:
        copy.wait()


def local(features, stale_store, serve_rows, neighbours, degrees, push_rows, weight, cotangent):
    rows, width = features.shape
    stores = stale_store.shape[0]
    nw, nz = NY * NX * NC, 12
    cw = width // NCH
    any_, vmem = pl.BlockSpec(memory_space=pl.ANY), pl.BlockSpec(memory_space=pltpu.VMEM)
    dma = pltpu.SemaphoreType.DMA
    V = pltpu.VMEM
    shapes = (
        jax.ShapeDtypeStruct((stores, width), BF16),
        jax.ShapeDtypeStruct((width // nw, width), F32),
    )
    made = pl.pallas_call(
        kernel,
        out_shape=shapes,
        in_specs=[any_, any_, vmem, vmem, vmem, vmem, any_, any_],
        out_specs=(any_, vmem),
        scratch_shapes=[
            V((stores, width), BF16),
            V((rows, width), BF16),
            V((width, width), BF16),
            V((rows, width), BF16),
            V((NX, NY * NC * 8, stores), BF16),
            V((NX, NY, NC, 8, width), BF16),
            V((NX, NC, NY, 8, width), BF16),
            V((NX * NC, NY, 8, width), BF16),
            V((rows, nw * 8), BF16),
            V((rows, width), F32),
            V((rows, 128), F32),
            V((stores, rows), BF16),
            V((rows, width), BF16),
            V((nw // NC, NC, 16, rows), BF16),
            V((nw // NC, 16, rows), BF16),
            V((rows, width), BF16),
            V((NCH, rows, cw), BF16),
            V((NCH, rows, cw), BF16),
            V((NCH, NY, NX, 16, cw), F32),
            V((NCH, NX, NY, 16, cw), BF16),
            V((NCH, NX, NY, 16, cw), BF16),
            V((NCH, NY, 16, cw), BF16),
            V((NCH, NY, 16, cw), BF16),
            V((NCH, nz, 16, cw), BF16),
            V((stores, width), BF16),
            dma((4,)),
            dma((NX, NY)),
            dma((NX, NY)),
            dma((NX * NC,)),
            dma((NX * NC,)),
            dma((NCH + 1,)),
            dma((NCH + 1,)),
            dma((NCH, NX)),
            dma((NCH, NX)),
            dma((NCH, NY)),
            dma((NCH, NY)),
            dma((NCH, nz)),
            dma((NCH, nz)),
            dma(()),
        ],
        compiler_params=pltpu.CompilerParams(
            collective_id=0, has_side_effects=True, vmem_limit_bytes=56 * 2**20
        ),
        cost_estimate=pl.CostEstimate(flops=6 * 10**9, bytes_accessed=6 * 2**20, transcendentals=2**20),
        name="sage",
    )(
        features, stale_store, serve_rows.T, neighbours.T, degrees.reshape(1, rows),
        push_rows.reshape(1, stores), weight, cotangent,
    )
    return pl.pallas_call(
        finish, out_shape=shapes, in_specs=[vmem, vmem], out_specs=(any_, any_),
        scratch_shapes=[dma((2,))], name="finish",
    )(*made)


def solution(mesh):
    both = P(("wide", "narrow"), None)
    flat = P(("wide", "narrow"))
    return jax.shard_map(
        local, mesh=mesh, in_specs=(both, both, both, both, flat, flat, P(), both),
        out_specs=(both, P("wide", None)), check_vma=False,
    )
```

```python
import functools
import math

import jax
import jax.numpy as jnp
from jax import lax
from jax.experimental import pallas as pl
from jax.experimental.pallas import tpu as pltpu
from jax.sharding import PartitionSpec as P

MESH = pl.DeviceIdType.MESH
F32 = jnp.float32
BF16 = jnp.bfloat16

NY, NX, NC = 8, 4, 2
TILE = 128
CHUNKS = ((0, 2), (2, 2), (4, 2), (6, 2))
NCH = len(CHUNKS)
SPLIT = (0, 1)
FIRST = 2
SCALE = 1.0 / math.sqrt(393216)


def iota(shape, dim):
    return lax.broadcasted_iota(jnp.int32, shape, dim)


def kernel(
    features, store, serve_t, neigh_t, degrees, push, weight, cotangent,
    refreshed, grad_out,
    store_v, feat_v, weight_v, cot_v, pick, outgoing, staged, pulled, a_pull, acc, cols_v, push_v,
    agg, agg_t, agg_t_peer, out_v, dz, dz_peer, part,
    x_send, x_recv, y_send, y_recv, z_recv, tile_send, tile_recv, whole, refreshed_v,
    in_sem, pull_s, pull_r, relay_s, relay_r, core_s, core_r, xs, xr, ys, yr, zs, zr, ss, sr, ws, wr, out_sem, ready,
):
    w = lax.axis_index("wide")
    n = lax.axis_index("narrow")
    nw, nz = NY * NX * NC, 12
    y, x, c = w // (NX * NC), (w // NC) % NX, w % NC
    rows, width = feat_v.shape
    tiles = width // TILE

    barrier = pltpu.get_barrier_semaphore()

    def at_y(d):
        return (((y + d) % NY * NX + x) * NC + c, n)

    def at_xc(dx, dc):
        return ((y * NX + (x + dx) % NX) * NC + (c + dc) % NC, n)

    far_x, far_y = (2, 1, 3), (4, 3, 5, 2, 6, 1, 7)
    far_z = (6, 5, 7, 4, 8, 3, 9, 2, 10, 1, 11)
    plane = [at_y(d) for d in far_y]
    plane += [at_xc(dx, dc) for dx in range(NX) for dc in range(NC) if dx or dc]
    for device in plane:
        pl.semaphore_signal(barrier, inc=1, device_id=device, device_id_type=MESH)

    @pl.loop(n + 1, nz)
    def _(pz):
        pl.semaphore_signal(barrier, inc=1, device_id=(w, pz), device_id_type=MESH)

    loads = [
        pltpu.make_async_copy(src, dst, in_sem.at[i])
        for i, (src, dst) in enumerate(
            [(store, store_v), (features, feat_v), (weight, weight_v), (cotangent, cot_v)]
        )
    ]
    for load in loads:
        load.start()

    slots = nw * 8
    tiled = jnp.tile(serve_t[...].astype(F32), (nw, 1))
    s = iota((slots, nw), 0)
    reader = ((s // 16) % NY * NX + s // (NY * 16)) * NC + (s // 8) % NC
    wanted = jnp.sum(jnp.where(iota((slots, nw), 1) == reader, tiled, 0.0), axis=1, keepdims=True)
    hot = wanted.astype(jnp.int32) == iota((slots, store_v.shape[0]), 1)
    pick[...] = hot.astype(F32).astype(BF16).reshape(pick.shape)
    loads[0].wait()

    rounds = (2, 1, 3, 0)

    def pull_copy(r, d, there):
        px, py = (x + rounds[r]) % NX, (y + d) % NY
        to = y if there else py
        return pltpu.make_async_remote_copy(
            src_ref=outgoing.at[px, py], dst_ref=staged.at[px, :, to],
            send_sem=pull_s.at[r, py], recv_sem=pull_r.at[r, to],
            device_id=at_y(d), device_id_type=MESH,
        )

    def relay_copy(dx, dc, there):
        px, pc = (x + dx) % NX, (c + dc) % NC
        to = x * NC + c if there else px * NC + pc
        return pltpu.make_async_remote_copy(
            src_ref=staged.at[px, pc], dst_ref=pulled.at[to],
            send_sem=relay_s.at[px * NC + pc], recv_sem=relay_r.at[to],
            device_id=at_xc(dx, dc), device_id_type=MESH,
        )

    def serve(r):
        px = (x + rounds[r]) % NX
        rows_out = jnp.dot(pick[px], store_v[...], preferred_element_type=F32).astype(BF16)
        outgoing[px] = rows_out.reshape(NY, NC, 8, width)
        if r == 0:
            pl.semaphore_wait(barrier, len(plane) + n)
        for d in far_y:
            pull_copy(r, d, True).start()
        staged[px, :, y] = outgoing[px, y]

    def relay(r):
        for d in far_y:
            pull_copy(r, d, False).wait_recv()
        dx = rounds[r]
        for dc in range(NC):
            if dx or dc:
                relay_copy(dx, dc, True).start()
            else:
                pulled[x * NC + c] = staged[x, c]

    for r in range(FIRST):
        serve(r)

    @pl.loop(0, n)
    def _(pz):
        pl.semaphore_signal(ready, inc=1, device_id=(w, pz), device_id_type=MESH)

    deg = degrees[...]
    live = iota((8, rows), 0) < deg
    idx = jnp.where(live, neigh_t[...], -1).astype(F32)
    deg1 = jnp.broadcast_to(deg.astype(F32) + 1.0, (8, rows))
    pushed = jnp.concatenate([push[...].astype(F32)] * 2, axis=1)
    pushed = jnp.broadcast_to(pushed, (8, rows))
    stacked = jnp.concatenate([idx, deg1, pushed, jnp.zeros((104, rows), F32)], axis=0)
    cols_v[...] = stacked.T
    loads[1].wait()

    step = 64
    at = iota((step, slots), 1)
    named = rows + (at // 8 % NY * (NX * NC) + at // (8 * NY)) * 8 + at % 8

    @pl.loop(0, rows // step)
    def _(b):
        r = pl.ds(pl.multiple_of(b * step, step), step)
        cols = cols_v[r, :].astype(jnp.int32)
        near = jnp.zeros((step, rows), F32)
        far = jnp.zeros((step, slots), F32)
        for k in range(8):
            col = cols[:, k : k + 1]
            near = near + (col == iota((step, rows), 1)).astype(F32)
            far = far + (col == named).astype(F32)
        a_pull[r, :] = far.astype(BF16)
        acc[r, :] = feat_v[r, :].astype(F32) + jnp.dot(
            near.astype(BF16), feat_v[...], preferred_element_type=F32
        )

    push_v[...] = (
        (cols_v[0 : push_v.shape[0], 16:17].astype(jnp.int32) == iota(push_v.shape, 1)).astype(F32).astype(BF16)
    )
    loads[2].wait()
    loads[3].wait()

    for r in range(NX):
        relay(r)
        if r + FIRST < NX:
            serve(r + FIRST)
    for dx in range(NX):
        for dc in range(NC):
            if dx or dc:
                relay_copy(dx, dc, False).wait_recv()

    total = acc[...] + jnp.dot(
        a_pull[...], pulled[...].reshape(slots, width), preferred_element_type=F32
    )
    agg[...] = (total / cols_v[:, 8:9]).astype(BF16)
    agg_t[...] = agg[...].T.reshape(nw // NC, NC, 16, rows)

    other = (y * NX + x) * NC + 1 - c

    def core_copy(src, dst, i):
        return pltpu.make_async_remote_copy(
            src_ref=src, dst_ref=dst, send_sem=core_s.at[i], recv_sem=core_r.at[i],
            device_id=(other, n), device_id_type=MESH,
        )

    def columns(h):
        t, k = CHUNKS[h]
        return pl.ds(t * TILE, k * TILE)

    def span(h):
        return pl.ds(*CHUNKS[h])

    core = [core_copy(dz.at[:, columns(h)], dz_peer.at[:, columns(h)], h) for h in range(NCH)]
    core.append(core_copy(agg_t.at[:, 1 - c], agg_t_peer, NCH))
    core[NCH].start()

    def x_copy(h, d, there):
        px = (x + d) % NX
        to = x if there else px
        return pltpu.make_async_remote_copy(
            src_ref=x_send.at[px, span(h)], dst_ref=x_recv.at[to, span(h)],
            send_sem=xs.at[h, px], recv_sem=xr.at[h, to],
            device_id=at_xc(d, 0), device_id_type=MESH,
        )

    def y_copy(h, d, there):
        py = (y + d) % NY
        to = y if there else py
        return pltpu.make_async_remote_copy(
            src_ref=y_send.at[py, span(h)], dst_ref=y_recv.at[to, span(h)],
            send_sem=ys.at[h, py], recv_sem=yr.at[h, to],
            device_id=at_y(d), device_id_type=MESH,
        )

    def z_copy(h, d, there):
        pz = (n + d) % nz
        to = n if there else pz
        return pltpu.make_async_remote_copy(
            src_ref=z_recv.at[n, span(h)], dst_ref=z_recv.at[to, span(h)],
            send_sem=zs.at[h, pz], recv_sem=zr.at[h, to],
            device_id=(w, pz), device_id_type=MESH,
        )

    def owner(t):
        return (t * 3) // 2

    def split(h):
        return range(CHUNKS[h][0], sum(CHUNKS[h]))

    def tile_copy(t, sender):
        return pltpu.make_async_remote_copy(
            src_ref=tile_send.at[t], dst_ref=tile_recv.at[sender], send_sem=ss.at[t], recv_sem=sr.at[sender],
            device_id=(w, owner(t)), device_id_type=MESH,
        )

    def whole_copy(t, pz):
        return pltpu.make_async_remote_copy(
            src_ref=whole.at[t], dst_ref=whole.at[t], send_sem=ws.at[pz], recv_sem=wr.at[t],
            device_id=(w, pz), device_id_type=MESH,
        )

    def forward(h):
        at = columns(h)
        z = jnp.dot(agg[...], weight_v[:, at], preferred_element_type=F32)
        s = jax.nn.sigmoid(z)
        dz[:, at] = (cot_v[:, at].astype(F32) * s * (1.0 + z * (1.0 - s))).astype(BF16)
        core[h].start()
        out_v[:, at] = (z * s).astype(BF16)

    def backward(h):
        at = columns(h)
        if h == 0:
            core[NCH].wait_recv()
        g = jnp.dot(agg_t[:, c].reshape(rows, rows), dz[:, at], preferred_element_type=F32)
        core[h].wait_recv()
        g = g + jnp.dot(agg_t_peer[...].reshape(rows, rows), dz_peer[:, at], preferred_element_type=F32)
        for i, t in enumerate(split(h)):
            tile = g[:, i * TILE : (i + 1) * TILE].reshape(NY, NX, 16, TILE)
            part[t] = tile
            for k in range(NX):
                x_send[k, t] = tile[:, k].astype(BF16)
        for d in far_x:
            x_copy(h, d, True).start()

    def after_x(h):
        for d in far_x:
            x_copy(h, d, False).wait_recv()
        for t in split(h):
            total = part[t, :, x]
            for d in far_x:
                total = total + x_recv[(x + d) % NX, t].astype(F32)
            part[t, :, 0] = total
            for k in range(NY):
                y_send[k, t] = total[k].astype(BF16)
        for d in far_y:
            y_copy(h, d, True).start()

    def after_y(h):
        for d in far_y:
            y_copy(h, d, False).wait_recv()
        for t in split(h):
            total = part[t, y, 0]
            for d in far_y:
                total = total + y_recv[(y + d) % NY, t].astype(F32)
            if h not in SPLIT:
                z_recv[n, t] = total.astype(BF16)
                continue
            tile_send[t] = total.astype(BF16)

            @pl.when(n == owner(t))
            def _():
                tile_recv[n] = tile_send[t]

            @pl.when(n != owner(t))
            def _():
                tile_copy(t, n).start()

        if h not in SPLIT:
            for d in far_z:
                z_copy(h, d, True).start()

    def after_split(h):
        for t in split(h):

            @pl.when(n == owner(t))
            def _():
                @pl.loop(1, nz)
                def _(d):
                    tile_copy(t, (n + d) % nz).wait_recv()

                total = tile_recv[0].astype(F32)
                for k in range(1, nz):
                    total = total + tile_recv[k].astype(F32)
                whole[t] = total * F32(SCALE)
                for d in far_z:
                    whole_copy(t, (n + d) % nz).start()

    def after_z(h):
        if h not in SPLIT:
            for d in far_z:
                z_copy(h, d, False).wait_recv()
        for t in split(h):
            if h in SPLIT:

                @pl.when(n != owner(t))
                def _():
                    whole_copy(t, n).wait_recv()

                total = whole[t]
            else:
                total = z_recv[0, t].astype(F32)
                for k in range(1, nz):
                    total = total + z_recv[k, t].astype(F32)
                total = total * F32(SCALE)
            grad_out[:, pl.ds(t * TILE, TILE)] = total

    forward(0)
    for h in range(1, NCH):
        forward(h)
        backward(h - 1)
    backward(NCH - 1)

    for h in range(NCH):
        at = columns(h)
        refreshed_v[:, at] = jnp.dot(
            push_v[...], out_v[:, at], preferred_element_type=F32
        ).astype(BF16)
        if h == 0:
            after_x(0)
    store_back = pltpu.make_async_copy(refreshed_v, refreshed, out_sem)
    store_back.start()
    @pl.when(n < nz - 1)
    def _():
        pl.semaphore_wait(ready, nz - 1 - n)


    for h in range(1, NCH):
        after_x(h)
        after_y(h - 1)
    for r in range(NX):
        for d in far_y:
            pull_copy(r, d, True).wait_send()
    for dx in range(NX):
        for dc in range(NC):
            if dx or dc:
                relay_copy(dx, dc, True).wait_send()
    after_y(NCH - 1)
    for h in SPLIT:
        after_split(h)
    for copy in core:
        copy.wait_send()
    for h in range(NCH):
        for d in far_x:
            x_copy(h, d, True).wait_send()
        for d in far_y:
            y_copy(h, d, True).wait_send()
    store_back.wait()
    for h in range(NCH):
        after_z(h)
    for h in range(NCH):
        if h not in SPLIT:
            for d in far_z:
                z_copy(h, d, True).wait_send()
            continue
        for t in split(h):

            @pl.when(n != owner(t))
            def _():
                tile_copy(t, n).wait_send()

            @pl.when(n == owner(t))
            def _():
                @pl.loop(1, nz)
                def _(d):
                    whole_copy(t, (n + d) % nz).wait_send()


def finish(refreshed, grad, refreshed_out, grad_out, sem):
    copies = [
        pltpu.make_async_copy(refreshed, refreshed_out, sem.at[0]),
        pltpu.make_async_copy(grad, grad_out, sem.at[1]),
    ]
    for copy in copies:
        copy.start()
    for copy in copies:
        copy.wait()


def local(features, stale_store, serve_rows, neighbours, degrees, push_rows, weight, cotangent):
    rows, width = features.shape
    stores = stale_store.shape[0]
    nw, nz = NY * NX * NC, 12
    tiles = width // TILE
    any_, vmem = pl.BlockSpec(memory_space=pl.ANY), pl.BlockSpec(memory_space=pltpu.VMEM)
    dma = pltpu.SemaphoreType.DMA
    V = pltpu.VMEM
    shapes = (
        jax.ShapeDtypeStruct((stores, width), BF16),
        jax.ShapeDtypeStruct((width // nw, width), F32),
    )
    made = pl.pallas_call(
        kernel,
        out_shape=shapes,
        in_specs=[any_, any_, vmem, vmem, vmem, vmem, any_, any_],
        out_specs=(any_, vmem),
        scratch_shapes=[
            V((stores, width), BF16),
            V((rows, width), BF16),
            V((width, width), BF16),
            V((rows, width), BF16),
            V((NX, NY * NC * 8, stores), BF16),
            V((NX, NY, NC, 8, width), BF16),
            V((NX, NC, NY, 8, width), BF16),
            V((NX * NC, NY, 8, width), BF16),
            V((rows, nw * 8), BF16),
            V((rows, width), F32),
            V((rows, 128), F32),
            V((stores, rows), BF16),
            V((rows, width), BF16),
            V((nw // NC, NC, 16, rows), BF16),
            V((nw // NC, 16, rows), BF16),
            V((rows, width), BF16),
            V((rows, width), BF16),
            V((rows, width), BF16),
            V((tiles, NY, NX, 16, TILE), F32),
            V((NX, tiles, NY, 16, TILE), BF16),
            V((NX, tiles, NY, 16, TILE), BF16),
            V((NY, tiles, 16, TILE), BF16),
            V((NY, tiles, 16, TILE), BF16),
            V((nz, tiles, 16, TILE), BF16),
            V((tiles, 16, TILE), BF16),
            V((nz, 16, TILE), BF16),
            V((tiles, 16, TILE), F32),
            V((stores, width), BF16),
            dma((4,)),
            dma((NX, NY)),
            dma((NX, NY)),
            dma((NX * NC,)),
            dma((NX * NC,)),
            dma((NCH + 1,)),
            dma((NCH + 1,)),
            dma((NCH, NX)),
            dma((NCH, NX)),
            dma((NCH, NY)),
            dma((NCH, NY)),
            dma((NCH, nz)),
            dma((NCH, nz)),
            dma((tiles,)),
            dma((nz,)),
            dma((nz,)),
            dma((tiles,)),
            dma(()),
            pltpu.SemaphoreType.REGULAR,
        ],
        compiler_params=pltpu.CompilerParams(
            collective_id=0, has_side_effects=True, vmem_limit_bytes=56 * 2**20
        ),
        cost_estimate=pl.CostEstimate(flops=6 * 10**9, bytes_accessed=6 * 2**20, transcendentals=2**20),
        name="sage",
    )(
        features, stale_store, serve_rows.T, neighbours.T, degrees.reshape(1, rows),
        push_rows.reshape(1, stores), weight, cotangent,
    )
    return pl.pallas_call(
        finish, out_shape=shapes, in_specs=[vmem, vmem], out_specs=(any_, any_),
        scratch_shapes=[dma((2,))], name="finish",
    )(*made)


def solution(mesh):
    both = P(("wide", "narrow"), None)
    flat = P(("wide", "narrow"))
    return jax.shard_map(
        local, mesh=mesh, in_specs=(both, both, both, both, flat, flat, P(), both),
        out_specs=(both, P("wide", None)), check_vma=False,
    )
```

```python
import functools
import math

import jax
import jax.numpy as jnp
from jax import lax
from jax.experimental import pallas as pl
from jax.experimental.pallas import tpu as pltpu
from jax.sharding import PartitionSpec as P

MESH = pl.DeviceIdType.MESH
F32 = jnp.float32
BF16 = jnp.bfloat16

NY, NX, NC = 8, 4, 2
TILE = 128
CHUNKS = ((0, 2), (2, 2), (4, 2), (6, 2))
NCH = len(CHUNKS)
SPLIT = (0, 1)
FIRST = 2
SCALE = 1.0 / math.sqrt(393216)


def iota(shape, dim):
    return lax.broadcasted_iota(jnp.int32, shape, dim)


def kernel(
    features, store, serve_t, neigh_t, degrees, push, weight, cotangent,
    refreshed, grad_out,
    store_v, feat_v, weight_v, cot_v, pick, outgoing, staged, pulled, a_pull, acc, cols_v, push_v,
    agg, agg_t, agg_t_peer, out_v, dz, dz_peer, part,
    x_send, x_recv, y_send, y_recv, z_recv, tile_send, tile_recv, whole, refreshed_v,
    in_sem, pull_s, pull_r, relay_s, relay_r, core_s, core_r, xs, xr, ys, yr, zs, zr, ss, sr, ws, wr, out_sem, ready,
):
    w = lax.axis_index("wide")
    n = lax.axis_index("narrow")
    nw, nz = NY * NX * NC, 12
    y, x, c = w // (NX * NC), (w // NC) % NX, w % NC
    rows, width = feat_v.shape
    tiles = width // TILE

    barrier = pltpu.get_barrier_semaphore()

    def at_y(d):
        return (((y + d) % NY * NX + x) * NC + c, n)

    def at_xc(dx, dc):
        return ((y * NX + (x + dx) % NX) * NC + (c + dc) % NC, n)

    far_x, far_y = (2, 1, 3), (4, 3, 5, 2, 6, 1, 7)
    far_z = (6, 5, 7, 4, 8, 3, 9, 2, 10, 1, 11)
    plane = [at_y(d) for d in far_y]
    plane += [at_xc(dx, dc) for dx in range(NX) for dc in range(NC) if dx or dc]
    for device in plane:
        pl.semaphore_signal(barrier, inc=1, device_id=device, device_id_type=MESH)

    @pl.loop(n + 1, nz)
    def _(pz):
        pl.semaphore_signal(barrier, inc=1, device_id=(w, pz), device_id_type=MESH)

    loads = [
        pltpu.make_async_copy(src, dst, in_sem.at[i])
        for i, (src, dst) in enumerate(
            [(store, store_v), (features, feat_v), (weight, weight_v), (cotangent, cot_v)]
        )
    ]
    for load in loads:
        load.start()

    slots = nw * 8
    tiled = jnp.tile(serve_t[...].astype(F32), (nw, 1))
    s = iota((slots, nw), 0)
    reader = ((s // 16) % NY * NX + s // (NY * 16)) * NC + (s // 8) % NC
    wanted = jnp.sum(jnp.where(iota((slots, nw), 1) == reader, tiled, 0.0), axis=1, keepdims=True)
    hot = wanted.astype(jnp.int32) == iota((slots, store_v.shape[0]), 1)
    pick[...] = hot.astype(F32).astype(BF16).reshape(pick.shape)
    loads[0].wait()

    rounds = (2, 1, 3, 0)

    def pull_copy(r, d, there):
        px, py = (x + rounds[r]) % NX, (y + d) % NY
        to = y if there else py
        return pltpu.make_async_remote_copy(
            src_ref=outgoing.at[px, py], dst_ref=staged.at[px, to],
            send_sem=pull_s.at[r, py], recv_sem=pull_r.at[r, to],
            device_id=at_y(d), device_id_type=MESH,
        )

    def relay_copy(dx, dc, there):
        px, pc = (x + dx) % NX, (c + dc) % NC
        to = x * NC + c if there else px * NC + pc
        return pltpu.make_async_remote_copy(
            src_ref=staged.at[px, :, pc], dst_ref=pulled.at[to],
            send_sem=relay_s.at[px * NC + pc], recv_sem=relay_r.at[to],
            device_id=at_xc(dx, dc), device_id_type=MESH,
        )

    def serve(r):
        px = (x + rounds[r]) % NX
        rows_out = jnp.dot(pick[px], store_v[...], preferred_element_type=F32).astype(BF16)
        outgoing[px] = rows_out.reshape(NY, NC, 8, width)
        if r == 0:
            pl.semaphore_wait(barrier, len(plane) + n)
        for d in far_y:
            pull_copy(r, d, True).start()
        staged[px, y] = outgoing[px, y]

    def relay(r):
        for d in far_y:
            pull_copy(r, d, False).wait_recv()
        dx = rounds[r]
        for dc in range(NC):
            if dx or dc:
                relay_copy(dx, dc, True).start()
            else:
                pulled[x * NC + c] = staged[x, :, c]

    for r in range(FIRST):
        serve(r)

    @pl.loop(0, n)
    def _(pz):
        pl.semaphore_signal(ready, inc=1, device_id=(w, pz), device_id_type=MESH)

    deg = degrees[...]
    live = iota((8, rows), 0) < deg
    idx = jnp.where(live, neigh_t[...], -1).astype(F32)
    deg1 = jnp.broadcast_to(deg.astype(F32) + 1.0, (8, rows))
    pushed = jnp.concatenate([push[...].astype(F32)] * 2, axis=1)
    pushed = jnp.broadcast_to(pushed, (8, rows))
    stacked = jnp.concatenate([idx, deg1, pushed, jnp.zeros((104, rows), F32)], axis=0)
    cols_v[...] = stacked.T
    loads[1].wait()

    step = 64
    at = iota((step, slots), 1)
    named = rows + (at // 8 % NY * (NX * NC) + at // (8 * NY)) * 8 + at % 8

    @pl.loop(0, rows // step)
    def _(b):
        r = pl.ds(pl.multiple_of(b * step, step), step)
        cols = cols_v[r, :].astype(jnp.int32)
        near = jnp.zeros((step, rows), F32)
        far = jnp.zeros((step, slots), F32)
        for k in range(8):
            col = cols[:, k : k + 1]
            near = near + (col == iota((step, rows), 1)).astype(F32)
            far = far + (col == named).astype(F32)
        a_pull[r, :] = far.astype(BF16)
        acc[r, :] = feat_v[r, :].astype(F32) + jnp.dot(
            near.astype(BF16), feat_v[...], preferred_element_type=F32
        )

    push_v[...] = (
        (cols_v[0 : push_v.shape[0], 16:17].astype(jnp.int32) == iota(push_v.shape, 1)).astype(F32).astype(BF16)
    )
    loads[2].wait()
    loads[3].wait()

    for r in range(NX):
        relay(r)
        if r + FIRST < NX:
            serve(r + FIRST)
    for dx in range(NX):
        for dc in range(NC):
            if dx or dc:
                relay_copy(dx, dc, False).wait_recv()

    total = acc[...] + jnp.dot(
        a_pull[...], pulled[...].reshape(slots, width), preferred_element_type=F32
    )
    agg[...] = (total / cols_v[:, 8:9]).astype(BF16)
    agg_t[...] = agg[...].T.reshape(nw // NC, NC, 16, rows)

    other = (y * NX + x) * NC + 1 - c

    def core_copy(src, dst, i):
        return pltpu.make_async_remote_copy(
            src_ref=src, dst_ref=dst, send_sem=core_s.at[i], recv_sem=core_r.at[i],
            device_id=(other, n), device_id_type=MESH,
        )

    def columns(h):
        t, k = CHUNKS[h]
        return pl.ds(t * TILE, k * TILE)

    def span(h):
        return pl.ds(*CHUNKS[h])

    core = [core_copy(dz.at[:, columns(h)], dz_peer.at[:, columns(h)], h) for h in range(NCH)]
    core.append(core_copy(agg_t.at[:, 1 - c], agg_t_peer, NCH))
    core[NCH].start()

    def x_copy(h, d, there):
        px = (x + d) % NX
        to = x if there else px
        return pltpu.make_async_remote_copy(
            src_ref=x_send.at[px, span(h)], dst_ref=x_recv.at[to, span(h)],
            send_sem=xs.at[h, px], recv_sem=xr.at[h, to],
            device_id=at_xc(d, 0), device_id_type=MESH,
        )

    def y_copy(h, d, there):
        py = (y + d) % NY
        to = y if there else py
        return pltpu.make_async_remote_copy(
            src_ref=y_send.at[py, span(h)], dst_ref=y_recv.at[to, span(h)],
            send_sem=ys.at[h, py], recv_sem=yr.at[h, to],
            device_id=at_y(d), device_id_type=MESH,
        )

    def z_copy(h, d, there):
        pz = (n + d) % nz
        to = n if there else pz
        return pltpu.make_async_remote_copy(
            src_ref=z_recv.at[n, span(h)], dst_ref=z_recv.at[to, span(h)],
            send_sem=zs.at[h, pz], recv_sem=zr.at[h, to],
            device_id=(w, pz), device_id_type=MESH,
        )

    def owner(t):
        return t

    def split(h):
        return range(CHUNKS[h][0], sum(CHUNKS[h]))

    def tile_copy(t, sender):
        return pltpu.make_async_remote_copy(
            src_ref=tile_send.at[t], dst_ref=tile_recv.at[sender], send_sem=ss.at[t], recv_sem=sr.at[sender],
            device_id=(w, owner(t)), device_id_type=MESH,
        )

    def whole_copy(t, pz):
        return pltpu.make_async_remote_copy(
            src_ref=whole.at[t], dst_ref=whole.at[t], send_sem=ws.at[pz], recv_sem=wr.at[t],
            device_id=(w, pz), device_id_type=MESH,
        )

    def forward(h):
        at = columns(h)
        z = jnp.dot(agg[...], weight_v[:, at], preferred_element_type=F32)
        s = jax.nn.sigmoid(z)
        dz[:, at] = (cot_v[:, at].astype(F32) * s * (1.0 + z * (1.0 - s))).astype(BF16)
        core[h].start()
        out_v[:, at] = (z * s).astype(BF16)

    def backward(h):
        at = columns(h)
        if h == 0:
            core[NCH].wait_recv()
        g = jnp.dot(agg_t[:, c].reshape(rows, rows), dz[:, at], preferred_element_type=F32)
        core[h].wait_recv()
        g = g + jnp.dot(agg_t_peer[...].reshape(rows, rows), dz_peer[:, at], preferred_element_type=F32)
        for i, t in enumerate(split(h)):
            tile = g[:, i * TILE : (i + 1) * TILE].reshape(NY, NX, 16, TILE)
            part[t] = tile
            for k in range(NX):
                x_send[k, t] = tile[:, k].astype(BF16)
        for d in far_x:
            x_copy(h, d, True).start()

    def after_x(h):
        for d in far_x:
            x_copy(h, d, False).wait_recv()
        for t in split(h):
            total = part[t, :, x]
            for d in far_x:
                total = total + x_recv[(x + d) % NX, t].astype(F32)
            part[t, :, 0] = total
            for k in range(NY):
                y_send[k, t] = total[k].astype(BF16)
        for d in far_y:
            y_copy(h, d, True).start()

    def after_y(h):
        for d in far_y:
            y_copy(h, d, False).wait_recv()
        for t in split(h):
            total = part[t, y, 0]
            for d in far_y:
                total = total + y_recv[(y + d) % NY, t].astype(F32)
            if h not in SPLIT:
                z_recv[n, t] = total.astype(BF16)
                continue
            tile_send[t] = total.astype(BF16)

            @pl.when(n == owner(t))
            def _():
                tile_recv[n] = tile_send[t]

            @pl.when(n != owner(t))
            def _():
                tile_copy(t, n).start()

        if h not in SPLIT:
            for d in far_z:
                z_copy(h, d, True).start()

    def after_split(h):
        for t in split(h):

            @pl.when(n == owner(t))
            def _():
                @pl.loop(1, nz)
                def _(d):
                    tile_copy(t, (n + d) % nz).wait_recv()

                total = tile_recv[0].astype(F32)
                for k in range(1, nz):
                    total = total + tile_recv[k].astype(F32)
                whole[t] = total * F32(SCALE)
                for d in far_z:
                    whole_copy(t, (n + d) % nz).start()

    def after_z(h):
        if h not in SPLIT:
            for d in far_z:
                z_copy(h, d, False).wait_recv()
        for t in split(h):
            if h in SPLIT:

                @pl.when(n != owner(t))
                def _():
                    whole_copy(t, n).wait_recv()

                total = whole[t]
            else:
                total = z_recv[0, t].astype(F32)
                for k in range(1, nz):
                    total = total + z_recv[k, t].astype(F32)
                total = total * F32(SCALE)
            grad_out[:, pl.ds(t * TILE, TILE)] = total

    forward(0)
    for h in range(1, NCH):
        forward(h)
        backward(h - 1)
    backward(NCH - 1)

    for h in range(NCH):
        at = columns(h)
        refreshed_v[:, at] = jnp.dot(
            push_v[...], out_v[:, at], preferred_element_type=F32
        ).astype(BF16)
        if h == 0:
            after_x(0)
    store_back = pltpu.make_async_copy(refreshed_v, refreshed, out_sem)
    store_back.start()
    @pl.when(n < nz - 1)
    def _():
        pl.semaphore_wait(ready, nz - 1 - n)


    for h in range(1, NCH):
        after_x(h)
        after_y(h - 1)
    for r in range(NX):
        for d in far_y:
            pull_copy(r, d, True).wait_send()
    for dx in range(NX):
        for dc in range(NC):
            if dx or dc:
                relay_copy(dx, dc, True).wait_send()
    after_y(NCH - 1)
    for h in SPLIT:
        after_split(h)
    for copy in core:
        copy.wait_send()
    for h in range(NCH):
        for d in far_x:
            x_copy(h, d, True).wait_send()
        for d in far_y:
            y_copy(h, d, True).wait_send()
    store_back.wait()
    for h in range(NCH):
        after_z(h)
    for h in range(NCH):
        if h not in SPLIT:
            for d in far_z:
                z_copy(h, d, True).wait_send()
            continue
        for t in split(h):

            @pl.when(n != owner(t))
            def _():
                tile_copy(t, n).wait_send()

            @pl.when(n == owner(t))
            def _():
                @pl.loop(1, nz)
                def _(d):
                    whole_copy(t, (n + d) % nz).wait_send()


def finish(refreshed, grad, refreshed_out, grad_out, sem):
    copies = [
        pltpu.make_async_copy(refreshed, refreshed_out, sem.at[0]),
        pltpu.make_async_copy(grad, grad_out, sem.at[1]),
    ]
    for copy in copies:
        copy.start()
    for copy in copies:
        copy.wait()


def local(features, stale_store, serve_rows, neighbours, degrees, push_rows, weight, cotangent):
    rows, width = features.shape
    stores = stale_store.shape[0]
    nw, nz = NY * NX * NC, 12
    tiles = width // TILE
    any_, vmem = pl.BlockSpec(memory_space=pl.ANY), pl.BlockSpec(memory_space=pltpu.VMEM)
    dma = pltpu.SemaphoreType.DMA
    V = pltpu.VMEM
    shapes = (
        jax.ShapeDtypeStruct((stores, width), BF16),
        jax.ShapeDtypeStruct((width // nw, width), F32),
    )
    made = pl.pallas_call(
        kernel,
        out_shape=shapes,
        in_specs=[any_, any_, vmem, vmem, vmem, vmem, any_, any_],
        out_specs=(any_, vmem),
        scratch_shapes=[
            V((stores, width), BF16),
            V((rows, width), BF16),
            V((width, width), BF16),
            V((rows, width), BF16),
            V((NX, NY * NC * 8, stores), BF16),
            V((NX, NY, NC, 8, width), BF16),
            V((NX, NY, NC, 8, width), BF16),
            V((NX * NC, NY, 8, width), BF16),
            V((rows, nw * 8), BF16),
            V((rows, width), F32),
            V((rows, 128), F32),
            V((stores, rows), BF16),
            V((rows, width), BF16),
            V((nw // NC, NC, 16, rows), BF16),
            V((nw // NC, 16, rows), BF16),
            V((rows, width), BF16),
            V((rows, width), BF16),
            V((rows, width), BF16),
            V((tiles, NY, NX, 16, TILE), F32),
            V((NX, tiles, NY, 16, TILE), BF16),
            V((NX, tiles, NY, 16, TILE), BF16),
            V((NY, tiles, 16, TILE), BF16),
            V((NY, tiles, 16, TILE), BF16),
            V((nz, tiles, 16, TILE), BF16),
            V((tiles, 16, TILE), BF16),
            V((nz, 16, TILE), BF16),
            V((tiles, 16, TILE), F32),
            V((stores, width), BF16),
            dma((4,)),
            dma((NX, NY)),
            dma((NX, NY)),
            dma((NX * NC,)),
            dma((NX * NC,)),
            dma((NCH + 1,)),
            dma((NCH + 1,)),
            dma((NCH, NX)),
            dma((NCH, NX)),
            dma((NCH, NY)),
            dma((NCH, NY)),
            dma((NCH, nz)),
            dma((NCH, nz)),
            dma((tiles,)),
            dma((nz,)),
            dma((nz,)),
            dma((tiles,)),
            dma(()),
            pltpu.SemaphoreType.REGULAR,
        ],
        compiler_params=pltpu.CompilerParams(
            collective_id=0, has_side_effects=True, vmem_limit_bytes=56 * 2**20
        ),
        cost_estimate=pl.CostEstimate(flops=6 * 10**9, bytes_accessed=6 * 2**20, transcendentals=2**20),
        name="sage",
    )(
        features, stale_store, serve_rows.T, neighbours.T, degrees.reshape(1, rows),
        push_rows.reshape(1, stores), weight, cotangent,
    )
    return pl.pallas_call(
        finish, out_shape=shapes, in_specs=[vmem, vmem], out_specs=(any_, any_),
        scratch_shapes=[dma((2,))], name="finish",
    )(*made)


def solution(mesh):
    both = P(("wide", "narrow"), None)
    flat = P(("wide", "narrow"))
    return jax.shard_map(
        local, mesh=mesh, in_specs=(both, both, both, both, flat, flat, P(), both),
        out_specs=(both, P("wide", None)), check_vma=False,
    )
```
